512 devices in a mesh: section: 8 (over x, core), row: 8 (over y), col: 8 (over z).
Axes of the slice: x: 4, y: 8, z: 8, core: 2. Of those that a mesh axis runs over, the one named last changes fastest.
Arguments:
- tokens: bfloat16 [8, 512, 4096], P('section', ('row', 'col')), may hold values from -6 to 6
- gate_weight: bfloat16 [8, 4096, 14336], P('section', 'row', 'col'), may hold values from -0.09375 to 0.09375
- up_weight: bfloat16 [8, 4096, 14336], P('section', 'row', 'col'), may hold values from -0.09375 to 0.09375
Outputs:
- handed: bfloat16 [8, 512, 14336], P('section', ('row', 'col'))
The draws below stay inside these ranges and needn't reach their ends.
All inputs are finite; a program needn't handle non-finite values.
Results may differ from the reference program's by a relative error of at most 0.019.
Values may be sent and summed in bfloat16 or wider, within the bound.
A program may use at most 64 MiB of HBM per device.

```python
import jax
import jax.numpy as jnp
from jax import lax

D = 4096
FF = 14336
TOKENS = 512
SECTIONS = 8
N_ROW = 8


def shard_levels(stream_key, dims, shards, smallest, top_value):
    factor_of, own = 1.0, jax.random.fold_in(stream_key, 6)
    for position, blocks in shards:
        heights = jnp.exp(jax.random.uniform(jax.random.fold_in(own, position), (blocks,), jnp.float32, smallest / len(shards), top_value / len(shards)))
        factor_of = factor_of * jnp.repeat(heights, dims[position] // blocks).reshape([-1 if axis == position else 1 for axis in range(len(dims))])
    return factor_of


def bell_draw(own_key, extent, width, most, shards=(), dtype=jnp.bfloat16):
    array = width * jax.random.normal(own_key, extent, jnp.float32)
    if shards:
        array = array * shard_levels(own_key, extent, shards, -0.22, 0.18)
    return jnp.clip(array, -most, most).astype(dtype)


def setup_inputs(seed: int = 0) -> dict:
    key_list = jax.random.split(jax.random.key(seed), 4)
    return {
        "tokens": bell_draw(key_list[0], (SECTIONS, TOKENS, D), 1.0, 6.0, ((0, 8), (1, 64))),
        "gate_weight": bell_draw(key_list[1], (SECTIONS, D, FF), D ** -0.5, 0.09375, ((0, 8), (1, 8), (2, 8))),
        "up_weight": bell_draw(key_list[2], (SECTIONS, D, FF), D ** -0.5, 0.09375, ((0, 8), (1, 8), (2, 8))),
    }


def block_total(rows, weight):
    block_len = D // N_ROW
    total = jnp.zeros((rows.shape[0], weight.shape[1]), jnp.float32)
    for index in range(N_ROW):
        lower = index * block_len
        partial_value = jnp.dot(rows[:, lower:lower + block_len], weight[lower:lower + block_len, :], preferred_element_type=jnp.float32)
        partial_value = lax.optimization_barrier(partial_value.astype(jnp.bfloat16))
        total = total + partial_value.astype(jnp.float32)
    return total


def section_hidden(operands):
    rows, gate_w, up_w = operands
    gate_sum = block_total(rows, gate_w)
    up_sum = block_total(rows, up_w)
    return (jax.nn.silu(gate_sum) * up_sum).astype(jnp.bfloat16)


def reference(tokens, gate_weight, up_weight):
    hidden = lax.map(section_hidden, (tokens, gate_weight, up_weight))
    return jnp.roll(hidden, 1, axis=0)
```

```python
import functools

import jax
import jax.numpy as jnp
from jax import lax
from jax.experimental import pallas as pl
from jax.experimental.pallas import tpu as pltpu
from jax.sharding import PartitionSpec as P

MESH = pl.DeviceIdType.MESH
LANES = 128


def split_units(count, generations):
    sizes = [count // generations + (1 if i < count % generations else 0) for i in range(generations)]
    starts = [sum(sizes[:i]) for i in range(generations)]
    return list(zip(starts, sizes))


def kernel(sizes, tokens, gate, up, out, w, tk, tkm, rbuf, sbuf, hid, wsem, ysend, yrecv, zsend, zrecv, csem,
           rsend, rrecv, osend, orecv):
    n_sec, n_row, n_col, gens = sizes
    s, r, c = lax.axis_index("section"), lax.axis_index("row"), lax.axis_index("col")
    t_blk, depth = tk.shape[2], tk.shape[3]
    width = hid.shape[2]
    group = n_col * t_blk
    half = width // LANES // 2
    long, short = n_row // 2, n_row // 2 - 1
    nxt, prv = lax.rem(s + 1, n_sec), lax.rem(s + n_sec - 1, n_sec)

    def row_at(offset):
        return lax.rem(r + (offset % n_row), n_row)

    def col_at(offset):
        return lax.rem(c + (offset % n_col), n_col)

    def load_unit(u):
        cols = pl.ds(pl.multiple_of(u * LANES, LANES), LANES)
        left = pl.ds(pl.multiple_of(u * 2 * LANES, 2 * LANES), LANES)
        right = pl.ds(pl.multiple_of(u * 2 * LANES + LANES, LANES), LANES)
        pltpu.make_async_copy(gate.at[0, :, cols], w.at[:, left], wsem.at[u]).start()
        pltpu.make_async_copy(up.at[0, :, cols], w.at[:, right], wsem.at[u]).start()

    own = pltpu.make_async_copy(
        tokens.at[0, :, pl.ds(pl.multiple_of(r * depth, depth), depth)], tk.at[0, 0], csem)
    own.start()
    for start, size in gens:
        @pl.loop(start, start + size)
        def _(i):
            load_unit(i)
            load_unit(i + half)

    barrier = pltpu.get_barrier_semaphore()
    for o in range(1, n_row):
        pl.semaphore_signal(barrier, inc=1, device_id=(s, row_at(o), c), device_id_type=MESH)
    for q in range(1, n_col):
        pl.semaphore_signal(barrier, inc=1, device_id=(s, r, col_at(q)), device_id_type=MESH)
    for q in range(n_col):
        pl.semaphore_signal(barrier, inc=1, device_id=(prv, r, col_at(q)), device_id_type=MESH)
    pl.semaphore_wait(barrier, n_row - 1 + n_col - 1 + n_col)

    def y_copy(o):
        dest = row_at(-o)
        return pltpu.make_async_remote_copy(
            src_ref=tokens.at[0, :, pl.ds(pl.multiple_of(dest * depth, depth), depth)],
            dst_ref=tk.at[o, 0], send_sem=ysend, recv_sem=yrecv.at[o],
            device_id=(s, dest, c), device_id_type=MESH)

    def z_copy(o, q):
        return pltpu.make_async_remote_copy(
            src_ref=tk.at[o, 0], dst_ref=tk.at[o, q], send_sem=zsend, recv_sem=zrecv.at[o],
            device_id=(s, r, col_at(-q)), device_id_type=MESH)

    def spread(o):
        if o == 0:
            own.wait()
        else:
            y_copy(o).wait_recv()
        for q in range(1, n_col):
            z_copy(o, q).start()

    def gathered(o):
        block = tk.at[o, pl.ds(1, n_col - 1)]
        pltpu.make_async_remote_copy(
            src_ref=block, dst_ref=block, send_sem=zsend, recv_sem=zrecv.at[o],
            device_id=(s, r, col_at(1)), device_id_type=MESH).wait_recv()
        tkm[o] = tk[o].astype(jnp.float32).reshape(group, depth).astype(jnp.bfloat16)

    def product(o, u):
        cols = pl.ds(pl.multiple_of(u * 2 * LANES, 2 * LANES), 2 * LANES)
        return jnp.dot(tkm[o], w[:, cols], preferred_element_type=jnp.float32)

    order = []
    for d in range(long, 0, -1):
        order.append([d] if 2 * d == n_row else [d, n_row - d])
    for pair in order:
        for o in pair:
            y_copy(o).start()

    hops = []
    for k in range(1, long + 1):
        hops.append((True, k))
        if k <= short:
            hops.append((False, k))

    bases = {}
    total = 0
    for g, (start, size) in enumerate(gens):
        for hop in hops:
            bases[g, hop] = total
            total += size

    def lower(direction, is_long):
        return is_long == (direction == 0)

    def ring_copy(direction, index):
        return pltpu.make_async_remote_copy(
            src_ref=sbuf.at[direction, index], dst_ref=rbuf.at[direction, index],
            send_sem=rsend.at[direction], recv_sem=rrecv.at[direction, index],
            device_id=(s, row_at(1 if direction == 0 else -1), c), device_id_type=MESH)

    def received(direction, index):
        ring_copy(direction, index).wait_recv()
        return rbuf[direction, index].astype(jnp.float32)

    def slot(g, hop):
        start, size = gens[g]
        is_long, k = hop
        dist = (long if is_long else short) + 1 - k

        @pl.loop(0, size)
        def _(i):
            for direction in (0, 1):
                u = start + i + (0 if lower(direction, is_long) else half)
                o = dist if direction == 0 else n_row - dist
                if k == 1 and is_long:
                    cols = pl.ds(pl.multiple_of(u * 2 * LANES, 2 * LANES), 2 * LANES)
                    pltpu.make_async_copy(w.at[:, cols], w.at[:, cols], wsem.at[u]).wait()
                value = product(o, u)
                if k > 1:
                    value = value + received(direction, bases[g, (is_long, k - 1)] + i)
                index = bases[g, hop] + i
                sbuf[direction, index] = value.astype(jnp.bfloat16)
                ring_copy(direction, index).start()

    def out_copy(first, count, q):
        src = pl.ds(first * LANES, count * LANES)
        dst = pl.ds(pl.multiple_of(c * width + first * LANES, LANES), count * LANES)
        return pltpu.make_async_remote_copy(
            src_ref=hid.at[q, :, src], dst_ref=out.at[0, :, dst], send_sem=osend, recv_sem=orecv,
            device_id=(nxt, r, col_at(q)), device_id_type=MESH)

    def finish(g):
        start, size = gens[g]

        @pl.loop(0, size)
        def _(i):
            for is_lower in (True, False):
                u = start + i + (0 if is_lower else half)
                value = product(0, u)
                for direction in (0, 1):
                    is_long = is_lower == (direction == 0)
                    value = value + received(direction, bases[g, (is_long, long if is_long else short)] + i)
                gate_sum, up_sum = value[:, :LANES], value[:, LANES:]
                result = gate_sum / (1.0 + jnp.exp(-gate_sum)) * up_sum
                hid[:, :, pl.ds(pl.multiple_of(u * LANES, LANES), LANES)] = result.reshape(
                    n_col, t_blk, LANES).astype(jnp.bfloat16)

        for first in (start, start + half):
            for q in range(n_col):
                out_copy(first, size, q).start()

    for pair in order[:2]:
        for o in pair:
            spread(o)
    for g in range(len(gens)):
        for position, hop in enumerate(hops):
            if g == 0:
                is_long, k = hop
                if is_long:
                    if k == 1:
                        for o in order[0]:
                            gathered(o)
                elif k == 1:
                    for pair in order[2:]:
                        for o in pair:
                            spread(o)
                    spread(0)
                    for o in order[1]:
                        gathered(o)
                else:
                    for o in order[k]:
                        gathered(o)
            slot(g, hop)
            if position == 0 and g > 0:
                if g == 1:
                    gathered(0)
                finish(g - 1)
    if len(gens) == 1:
        gathered(0)
    finish(len(gens) - 1)

    def sent(block, sem):
        pltpu.make_async_remote_copy(
            src_ref=block, dst_ref=block, send_sem=sem, recv_sem=csem,
            device_id=(s, row_at(1), c), device_id_type=MESH).wait_send()

    sent(tk.at[pl.ds(0, n_row - 1), 0], ysend)
    sent(tk.at[:, pl.ds(0, n_col - 1)], zsend)
    for direction in (0, 1):
        sent(sbuf.at[direction], rsend.at[direction])
    sent(hid, osend)
    pltpu.make_async_remote_copy(
        src_ref=out, dst_ref=out, send_sem=osend, recv_sem=orecv,
        device_id=(nxt, r, c), device_id_type=MESH).wait_recv()


GENERATIONS = 2


def shards(tokens, gate_weight, up_weight):
    n_sec, n_row, n_col = (lax.axis_size(a) for a in ("section", "row", "col"))
    _, t_blk, _ = tokens.shape
    _, depth, width = gate_weight.shape
    units = width // LANES
    half = units // 2
    gens = split_units(half, GENERATIONS)
    group = n_col * t_blk
    slots = half * (n_row - 1)
    dma = pltpu.SemaphoreType.DMA
    return pl.pallas_call(
        functools.partial(kernel, (n_sec, n_row, n_col, gens)),
        out_shape=jax.ShapeDtypeStruct((1, t_blk, n_row_cols(width, n_col)), jnp.bfloat16),
        in_specs=[pl.BlockSpec(memory_space=pl.ANY)] * 3,
        out_specs=pl.BlockSpec(memory_space=pl.ANY),
        scratch_shapes=[
            pltpu.VMEM((depth, 2 * width), jnp.bfloat16),
            pltpu.VMEM((n_row, n_col, t_blk, depth), jnp.bfloat16),
            pltpu.VMEM((n_row, group, depth), jnp.bfloat16),
            pltpu.VMEM((2, slots, group, 2 * LANES), jnp.bfloat16),
            pltpu.VMEM((2, slots, group, 2 * LANES), jnp.bfloat16),
            pltpu.VMEM((n_col, t_blk, width), jnp.bfloat16),
            dma((units,)), dma, dma((n_row,)), dma, dma((n_row,)), dma,
            dma((2,)), dma((2, slots)), dma, dma,
        ],
        compiler_params=pltpu.CompilerParams(
            collective_id=0, has_side_effects=True, vmem_limit_bytes=48 * 1024 * 1024),
    )(tokens, gate_weight, up_weight)


def n_row_cols(width, n_col):
    return width * n_col


def solution(mesh):
    placed = (P("section", ("row", "col"), None), P("section", "row", "col"), P("section", "row", "col"))
    return jax.shard_map(
        shards, mesh=mesh, in_specs=placed, out_specs=P("section", ("row", "col"), None), check_vma=False)
```

```python
import functools

import jax
import jax.numpy as jnp
from jax import lax
from jax.experimental import pallas as pl
from jax.experimental.pallas import tpu as pltpu
from jax.sharding import PartitionSpec as P

MESH = pl.DeviceIdType.MESH
LANES = 128
UNIT = 2 * LANES
VMEM_MIB = 54
GENS = (7,)
EARLY = ((-2, 1), (0, 0), (-2, 2), (-1, 2), (-1, 3), (0, 1), (-2, 3), (-1, 4), (-1, 5), (0, 2), (-1, 6), (0, 3), (-1, -1))
LATE = ((0, 4), (0, 5), (0, 6), (0, -1))
SCHEDULE = EARLY + LATE


def kernel(plan, tokens, gate, up, out, tv, w, tk, tkm, p0, rb0, sb0, rbuf, sbuf, hid,
           wsem, tsem, ysend, yrecv, zsend, zrecv, esend, erecv, rsend, rrecv, osend, orecv):
    n_sec, n_row, n_col, gens, schedule = plan
    s, r, c = lax.axis_index("section"), lax.axis_index("row"), lax.axis_index("col")
    t_blk, depth = tk.shape[2], tk.shape[3]
    width = hid.shape[2]
    half = width // LANES // 2
    group = (n_col - 1) * t_blk
    long, short = n_row // 2, n_row // 2 - 1
    nxt, prv = lax.rem(s + 1, n_sec), lax.rem(s + n_sec - 1, n_sec)

    def row_at(offset):
        return lax.rem(r + (offset % n_row), n_row)

    def col_at(offset):
        return lax.rem(c + (offset % n_col), n_col)

    def unit_cols(u):
        return pl.ds(pl.multiple_of(u * UNIT, UNIT), UNIT)

    stage = pltpu.make_async_copy(tokens.at[0], tv, tsem)
    stage.start()
    barrier = pltpu.get_barrier_semaphore()
    for o in range(1, n_row):
        pl.semaphore_signal(barrier, inc=1, device_id=(s, row_at(o), c), device_id_type=MESH)
    for q in range(1, n_col):
        pl.semaphore_signal(barrier, inc=1, device_id=(s, r, col_at(q)), device_id_type=MESH)
    for q in range(n_col):
        pl.semaphore_signal(barrier, inc=1, device_id=(prv, r, col_at(q)), device_id_type=MESH)

    @pl.loop(0, 2 * half)
    def _(u):
        cols = pl.ds(pl.multiple_of(u * LANES, LANES), LANES)
        first = pl.ds(pl.multiple_of(u * UNIT, UNIT), LANES)
        second = pl.ds(pl.multiple_of(u * UNIT + LANES, LANES), LANES)
        pltpu.make_async_copy(gate.at[0, :, cols], w.at[:, first], wsem.at[u]).start()
        pltpu.make_async_copy(up.at[0, :, cols], w.at[:, second], wsem.at[u]).start()

    stage.wait()
    pl.semaphore_wait(barrier, n_row - 1 + n_col - 1 + n_col)

    batches = []
    for d in range(long, 0, -1):
        batches.append([d] if 2 * d == n_row else [d, n_row - d])
    batches[-1].append(0)
    flat = [o for batch in batches for o in batch]
    place = {o: i for i, o in enumerate(flat)}

    def y_copy(o):
        dest = row_at(-o)
        return pltpu.make_async_remote_copy(
            src_ref=tv.at[:, pl.ds(pl.multiple_of(dest * depth, depth), depth)], dst_ref=tk.at[0, place[o]],
            send_sem=ysend, recv_sem=yrecv.at[o], device_id=(s, dest, c), device_id_type=MESH)

    def z_range(b):
        return pl.ds(place[batches[b][0]], len(batches[b]))

    def z_send(b):
        for q in range(1, n_col):
            pltpu.make_async_remote_copy(
                src_ref=tk.at[0, z_range(b)], dst_ref=tk.at[q, z_range(b)], send_sem=zsend, recv_sem=zrecv.at[b],
                device_id=(s, r, col_at(-q)), device_id_type=MESH).start()

    def gathered(b):
        block = tk.at[pl.ds(1, n_col - 1), z_range(b)]
        pltpu.make_async_remote_copy(
            src_ref=block, dst_ref=block, send_sem=zsend, recv_sem=zrecv.at[b],
            device_id=(s, r, col_at(1)), device_id_type=MESH).wait_recv()
        for o in batches[b]:
            rows = tk[pl.ds(1, n_col - 1), place[o]].astype(jnp.float32)
            tkm[place[o]] = rows.reshape(group, depth).astype(jnp.bfloat16)

    for o in flat[:-1]:
        y_copy(o).start()
    own = pltpu.make_async_copy(tv.at[:, pl.ds(pl.multiple_of(r * depth, depth), depth)], tk.at[0, place[0]], tsem)
    own.start()

    hops = []
    for k in range(1, long + 1):
        hops.append((True, k))
        if k <= short:
            hops.append((False, k))

    def parity(direction, is_long):
        return 0 if is_long == (direction == 0) else 1

    def source(direction, hop):
        is_long, k = hop
        dist = (long if is_long else short) + 1 - k
        return dist if direction == 0 else n_row - dist

    def ring_to(direction):
        return (s, row_at(1 if direction == 0 else -1), c)

    def out_copy(first, count, q):
        src = pl.ds(pl.multiple_of(first * LANES, LANES), count * LANES)
        dst = pl.ds(pl.multiple_of(c * width + first * LANES, LANES), count * LANES)
        return pltpu.make_async_remote_copy(
            src_ref=hid.at[q, :, src], dst_ref=out.at[0, :, dst], send_sem=osend, recv_sem=orecv,
            device_id=(nxt, r, col_at(q)), device_id_type=MESH)

    def gated(value):
        gate_sum, up_sum = value[..., :LANES], value[..., LANES:]
        return gate_sum / (1.0 + jnp.exp(-gate_sum)) * up_sum

    def early_copy(direction, h):
        return pltpu.make_async_remote_copy(
            src_ref=sb0.at[direction, h], dst_ref=rb0.at[direction, h], send_sem=esend, recv_sem=erecv.at[direction, h],
            device_id=ring_to(direction), device_id_type=MESH)

    def early_hop(direction, h):
        is_long, k = hops[h]
        value = p0[parity(direction, is_long), :, place[source(direction, hops[h])]]
        if k > 1:
            before = hops.index((is_long, k - 1))
            early_copy(direction, before).wait_recv()
            value = value + rb0[direction, before].astype(jnp.float32)
        sb0[direction, h] = value.astype(jnp.bfloat16)
        early_copy(direction, h).start()

    def early_products(par):
        rows = tk[0].astype(jnp.float32).reshape(n_row * t_blk, depth).astype(jnp.bfloat16)

        @pl.loop(0, half)
        def _(i):
            u = 2 * i + par
            pltpu.make_async_copy(w.at[:, unit_cols(u)], w.at[:, unit_cols(u)], wsem.at[u]).wait()
            value = jnp.dot(rows, w[:, unit_cols(u)], preferred_element_type=jnp.float32)
            p0[par, i] = value.reshape(n_row, t_blk, UNIT)

    def early_finish():
        for par in (0, 1):
            value = p0[par, :, place[0]]
            for direction in (0, 1):
                is_long = (par == 0) == (direction == 0)
                h = hops.index((is_long, long if is_long else short))
                early_copy(direction, h).wait_recv()
                value = value + rb0[direction, h].astype(jnp.float32)
            result = gated(value)
            for i in range(half):
                u = 2 * i + par
                hid[0, :, u * LANES:(u + 1) * LANES] = result[i].astype(jnp.bfloat16)
        out_copy(0, 2 * half, 0).start()

    starts = [sum(gens[:g]) for g in range(len(gens))]
    bases = [[sum(gens[:g]) * len(hops) + h * gens[g] for h in range(len(hops))] for g in range(len(gens))]

    def ring_copy(direction, index):
        return pltpu.make_async_remote_copy(
            src_ref=sbuf.at[direction, index], dst_ref=rbuf.at[direction, index],
            send_sem=rsend.at[direction], recv_sem=rrecv.at[direction, index],
            device_id=ring_to(direction), device_id_type=MESH)

    def product(o, u):
        return jnp.dot(tkm[place[o]], w[:, unit_cols(u)], preferred_element_type=jnp.float32)

    def received(direction, index):
        ring_copy(direction, index).wait_recv()
        return rbuf[direction, index].astype(jnp.float32)

    def slot(g, h):
        is_long, k = hops[h]

        @pl.loop(0, gens[g])
        def _(i):
            for direction in (0, 1):
                value = product(source(direction, hops[h]), 2 * (starts[g] + i) + parity(direction, is_long))
                if k > 1:
                    value = value + received(direction, bases[g][hops.index((is_long, k - 1))] + i)
                index = bases[g][h] + i
                sbuf[direction, index] = value.astype(jnp.bfloat16)
                ring_copy(direction, index).start()

    def finish(g):
        @pl.loop(0, gens[g])
        def _(i):
            for par in (0, 1):
                u = 2 * (starts[g] + i) + par
                value = product(0, u)
                for direction in (0, 1):
                    is_long = (par == 0) == (direction == 0)
                    value = value + received(direction, bases[g][hops.index((is_long, long if is_long else short))] + i)
                hid[pl.ds(1, n_col - 1), :, pl.ds(pl.multiple_of(u * LANES, LANES), LANES)] = gated(value).reshape(
                    n_col - 1, t_blk, LANES).astype(jnp.bfloat16)
            for q in range(1, n_col):
                out_copy(2 * (starts[g] + i), 2, q).start()

    ready = set()

    def need(b):
        if b not in ready:
            ready.add(b)
            gathered(b)

    y_copy(flat[0]).wait_recv()
    z_send(0)
    for o in flat[1:-1]:
        y_copy(o).wait_recv()
    own.wait()
    early_products(0)
    early_hop(0, 0)
    early_hop(1, 1)
    early_products(1)
    early_hop(1, 0)
    early_hop(0, 1)
    for g, h in schedule:
        if g == -2:
            z_send(h)
        elif g < 0:
            if h < 0:
                early_finish()
            elif h > 1:
                for direction in (0, 1):
                    early_hop(direction, h)
        elif h < 0:
            finish(g)
        else:
            is_long, k = hops[h]
            need(k - 1 if is_long else k)
            slot(g, h)

    def sent(block, sem):
        pltpu.make_async_remote_copy(
            src_ref=block, dst_ref=block, send_sem=sem, recv_sem=tsem,
            device_id=ring_to(0), device_id_type=MESH).wait_send()

    sent(tk.at[0, pl.ds(0, n_row - 1)], ysend)
    sent(tk.at[pl.ds(1, n_col - 1)], zsend)
    sent(sb0, esend)
    for direction in (0, 1):
        sent(sbuf.at[direction], rsend.at[direction])
    sent(hid, osend)
    pltpu.make_async_remote_copy(
        src_ref=out, dst_ref=out, send_sem=osend, recv_sem=orecv,
        device_id=ring_to(0), device_id_type=MESH).wait_recv()


def shards(tokens, gate_weight, up_weight):
    n_sec, n_row, n_col = (lax.axis_size(a) for a in ("section", "row", "col"))
    _, t_blk, features = tokens.shape
    _, depth, width = gate_weight.shape
    units = width // LANES
    half = units // 2
    group = (n_col - 1) * t_blk
    n_hops = n_row - 1
    slots = half * n_hops
    dma = pltpu.SemaphoreType.DMA
    bf16 = jnp.bfloat16
    return pl.pallas_call(
        functools.partial(kernel, (n_sec, n_row, n_col, GENS, SCHEDULE)),
        out_shape=jax.ShapeDtypeStruct((1, t_blk, width * n_col), bf16),
        in_specs=[pl.BlockSpec(memory_space=pltpu.HBM)] * 3,
        out_specs=pl.BlockSpec(memory_space=pl.ANY),
        scratch_shapes=[
            pltpu.VMEM((t_blk, features), bf16),
            pltpu.VMEM((depth, 2 * width), bf16),
            pltpu.VMEM((n_col, n_row, t_blk, depth), bf16),
            pltpu.VMEM((n_row, group, depth), bf16),
            pltpu.VMEM((2, half, n_row, t_blk, UNIT), jnp.float32),
            pltpu.VMEM((2, n_hops, half, t_blk, UNIT), bf16),
            pltpu.VMEM((2, n_hops, half, t_blk, UNIT), bf16),
            pltpu.VMEM((2, slots, group, UNIT), bf16),
            pltpu.VMEM((2, slots, group, UNIT), bf16),
            pltpu.VMEM((n_col, t_blk, width), bf16),
            dma((units,)), dma, dma, dma((n_row,)), dma, dma((n_row,)), dma, dma((2, n_hops)),
            dma((2,)), dma((2, slots)), dma, dma,
        ],
        compiler_params=pltpu.CompilerParams(
            collective_id=0, has_side_effects=True, vmem_limit_bytes=VMEM_MIB * 1024 * 1024),
    )(tokens, gate_weight, up_weight)


def solution(mesh):
    placed = (P("section", ("row", "col"), None), P("section", "row", "col"), P("section", "row", "col"))
    return jax.shard_map(
        shards, mesh=mesh, in_specs=placed, out_specs=P("section", ("row", "col"), None), check_vma=False)
```

```python
import functools

import jax
import jax.numpy as jnp
from jax import lax
from jax.experimental import pallas as pl
from jax.experimental.pallas import tpu as pltpu
from jax.sharding import PartitionSpec as P

MESH = pl.DeviceIdType.MESH
LANES = 128
UNIT = 2 * LANES
VMEM_MIB = 54
PIECE = 2
LOW = 4
EARLY = ((-2, 1), (0, 0, 0, 7), (-2, 2), (-1, 2), (-1, 3), (1, 0, 0, 7), (-2, 3), (-1, 4), (-1, 5), (0, 1, 0, 7), (-1, 6), (1, 1, 0, 7), (-1, -1))
LATE = ((0, 2, 0, 7), (0, 3, 0, 7), (1, 2, 0, 7), (0, 4, 0, 7), (0, 5, 0, 7), (1, 3, 0, 7), (0, 6, 0, 7), (1, 4, 0, 7), (0, -1, 0, 7), (1, 5, 0, 4), (1, 6, 0, 4), (1, 5, 4, 3), (1, -1, 0, 4), (1, 6, 4, 3), (1, -1, 4, 3))
SCHEDULE = EARLY + LATE
EAGER = 2


def kernel(plan, tokens, gate, up, out, tv, w, tk, tkm, p0, rb0, sb0, kept, rlow, rhigh, slow, shigh, hid,
           wsem, tsem, ysend, yrecv, zsend, zrecv, esend, erecv, rsend, rrecv, osend, orecv, late, go):
    n_sec, n_row, n_col, schedule, eager, low, piece_units = plan
    s, r, c = lax.axis_index("section"), lax.axis_index("row"), lax.axis_index("col")
    t_blk, depth = tk.shape[2], tk.shape[3]
    width = hid.shape[2]
    half = width // LANES // 2
    group = (n_col - 1) * t_blk
    long, short = n_row // 2, n_row // 2 - 1
    nxt, prv = lax.rem(s + 1, n_sec), lax.rem(s + n_sec - 1, n_sec)

    def row_at(offset):
        return lax.rem(r + (offset % n_row), n_row)

    def col_at(offset):
        return lax.rem(c + (offset % n_col), n_col)

    last = n_col - 1

    def tell(sem, device):
        pl.semaphore_signal(sem, inc=1, device_id=device, device_id_type=MESH)

    def unit_cols(u):
        return pl.ds(pl.multiple_of(u * UNIT, UNIT), UNIT)

    stage = pltpu.make_async_copy(tokens.at[0], tv, tsem)
    stage.start()
    barrier = pltpu.get_barrier_semaphore()
    for o in range(1, n_row):
        tell(barrier, (s, row_at(o), c))
    for j in range(1, n_col):
        @pl.when(c < j)
        def _():
            tell(barrier, (s, r, j))

    @pl.when(c == last)
    def _():
        tell(barrier, (nxt, r, last))

    @pl.loop(0, 2 * half)
    def _(u):
        cols = pl.ds(pl.multiple_of(u * LANES, LANES), LANES)
        first = pl.ds(pl.multiple_of(u * UNIT, UNIT), LANES)
        second = pl.ds(pl.multiple_of(u * UNIT + LANES, LANES), LANES)
        pltpu.make_async_copy(gate.at[0, :, cols], w.at[:, first], wsem.at[u]).start()
        pltpu.make_async_copy(up.at[0, :, cols], w.at[:, second], wsem.at[u]).start()

    stage.wait()
    pl.semaphore_wait(barrier, n_row - 1 + c + jnp.where(c == last, 1, 0))

    for j in range(last):
        @pl.when(c > j)
        def _():
            tell(late, (s, r, j))

    @pl.when(c == last)
    def _():
        tell(go, (prv, r, last))

    batches = []
    for d in range(long, 0, -1):
        batches.append([d] if 2 * d == n_row else [d, n_row - d])
    batches[-1].append(0)
    flat = [o for batch in batches for o in batch]
    place = {o: i for i, o in enumerate(flat)}

    def y_copy(o):
        dest = row_at(-o)
        return pltpu.make_async_remote_copy(
            src_ref=tv.at[:, pl.ds(pl.multiple_of(dest * depth, depth), depth)], dst_ref=tk.at[0, place[o]],
            send_sem=ysend, recv_sem=yrecv.at[o], device_id=(s, dest, c), device_id_type=MESH)

    def z_range(b):
        return pl.ds(place[batches[b][0]], len(batches[b]))

    def z_send(b):
        for q in range(1, n_col):
            dest = col_at(-q)
            pltpu.make_async_remote_copy(
                src_ref=tk.at[0, z_range(b)], dst_ref=tk.at[jnp.where(c < dest, c + 1, c), z_range(b)],
                send_sem=zsend, recv_sem=zrecv.at[b], device_id=(s, r, dest), device_id_type=MESH).start()

    def gathered(b):
        block = tk.at[pl.ds(1, n_col - 1), z_range(b)]
        pltpu.make_async_remote_copy(
            src_ref=block, dst_ref=block, send_sem=zsend, recv_sem=zrecv.at[b],
            device_id=(s, r, col_at(1)), device_id_type=MESH).wait_recv()
        for o in batches[b]:
            rows = tk[pl.ds(1, n_col - 1), place[o]].astype(jnp.float32)
            tkm[place[o]] = rows.reshape(group, depth).astype(jnp.bfloat16)

    for o in flat[:-1]:
        y_copy(o).start()
    own = pltpu.make_async_copy(tv.at[:, pl.ds(pl.multiple_of(r * depth, depth), depth)], tk.at[0, place[0]], tsem)
    own.start()

    hops = []
    for k in range(1, long + 1):
        hops.append((True, k))
        if k <= short:
            hops.append((False, k))

    def parity(direction, is_long):
        return 0 if is_long == (direction == 0) else 1

    def source(direction, hop):
        is_long, k = hop
        dist = (long if is_long else short) + 1 - k
        return dist if direction == 0 else n_row - dist

    def ring_to(direction):
        return (s, row_at(1 if direction == 0 else -1), c)

    def out_copy(first, count, k):
        src = pl.ds(pl.multiple_of(first * LANES, LANES), count * LANES)
        dst = pl.ds(pl.multiple_of(c * width + first * LANES, LANES), count * LANES)
        return pltpu.make_async_remote_copy(
            src_ref=hid.at[k, :, src], dst_ref=out.at[0, :, dst], send_sem=osend, recv_sem=orecv,
            device_id=(nxt, r, c if k == 0 else jnp.where(k - 1 < c, k - 1, k)), device_id_type=MESH)

    def gated(value):
        gate_sum, up_sum = value[..., :LANES], value[..., LANES:]
        return gate_sum / (1.0 + jnp.exp(-gate_sum)) * up_sum

    def early_copy(direction, h):
        return pltpu.make_async_remote_copy(
            src_ref=sb0.at[direction, h], dst_ref=rb0.at[direction, h], send_sem=esend, recv_sem=erecv.at[direction, h],
            device_id=ring_to(direction), device_id_type=MESH)

    def early_hop(direction, h):
        is_long, k = hops[h]
        value = p0[parity(direction, is_long), :, place[source(direction, hops[h])]]
        if k > 1:
            before = hops.index((is_long, k - 1))
            early_copy(direction, before).wait_recv()
            value = value + rb0[direction, before].astype(jnp.float32)
        sb0[direction, h] = value.astype(jnp.bfloat16)
        early_copy(direction, h).start()

    def early_products(par):
        rows = tk[0].astype(jnp.float32).reshape(n_row * t_blk, depth).astype(jnp.bfloat16)

        @pl.loop(0, half)
        def _(i):
            u = 2 * i + par
            pltpu.make_async_copy(w.at[:, unit_cols(u)], w.at[:, unit_cols(u)], wsem.at[u]).wait()
            value = jnp.dot(rows, w[:, unit_cols(u)], preferred_element_type=jnp.float32)
            p0[par, i] = value.reshape(n_row, t_blk, UNIT)

    def early_finish():
        for par in (0, 1):
            value = p0[par, :, place[0]]
            for direction in (0, 1):
                is_long = (par == 0) == (direction == 0)
                h = hops.index((is_long, long if is_long else short))
                early_copy(direction, h).wait_recv()
                value = value + rb0[direction, h].astype(jnp.float32)
            result = gated(value)
            for i in range(half):
                u = 2 * i + par
                hid[0, :, u * LANES:(u + 1) * LANES] = result[i].astype(jnp.bfloat16)
        out_copy(0, 2 * half, 0).start()

    edge = low * t_blk
    cut = ((0, edge, slow, rlow), (edge, group - edge, shigh, rhigh))

    def ring_copy(part, direction, index, n):
        _, _, sbuf, rbuf = cut[part]
        return pltpu.make_async_remote_copy(
            src_ref=sbuf.at[direction, pl.ds(index, n)], dst_ref=rbuf.at[direction, pl.ds(index, n)],
            send_sem=rsend.at[direction, part], recv_sem=rrecv.at[direction, part, index],
            device_id=ring_to(direction), device_id_type=MESH)

    def product(part, o, u):
        if part == 1:
            return kept[place[o], u]
        value = jnp.dot(tkm[place[o]], w[:, unit_cols(u)], preferred_element_type=jnp.float32)
        kept[place[o], u] = value[edge:]
        return value[:edge]

    def by_pieces(first, count, do):
        whole = count // piece_units
        if whole:
            @pl.loop(0, whole)
            def _(j):
                do(first + j * piece_units, piece_units)
        if count % piece_units:
            do(first + whole * piece_units, count % piece_units)

    def slot(part, h, first, count):
        is_long, k = hops[h]
        _, _, sbuf, rbuf = cut[part]

        def do(i, n):
            for direction in (0, 1):
                here = h * half + i
                before = hops.index((is_long, k - 1)) * half + i if k > 1 else 0
                o = source(direction, hops[h])
                values = [product(part, o, 2 * (i + e) + parity(direction, is_long)) for e in range(n)]
                if k > 1:
                    ring_copy(part, direction, before, n).wait_recv()
                for e in range(n):
                    value = values[e]
                    if k > 1:
                        value = value + rbuf[direction, before + e].astype(jnp.float32)
                    sbuf[direction, here + e] = value.astype(jnp.bfloat16)
                ring_copy(part, direction, here, n).start()

        by_pieces(first, count, do)

    def finish(part, first, count):
        start, rows, _, rbuf = cut[part]
        places = range(1, 1 + low) if part == 0 else range(1 + low, n_col)

        def do(i, n):
            for par in (0, 1):
                values = [product(part, 0, 2 * (i + e) + par) for e in range(n)]
                for direction in (0, 1):
                    is_long = (par == 0) == (direction == 0)
                    before = hops.index((is_long, long if is_long else short)) * half + i
                    ring_copy(part, direction, before, n).wait_recv()
                    values = [values[e] + rbuf[direction, before + e].astype(jnp.float32) for e in range(n)]
                for e in range(n):
                    u = 2 * (i + e) + par
                    hid[pl.ds(places[0], len(places)), :, pl.ds(pl.multiple_of(u * LANES, LANES), LANES)] = gated(
                        values[e]).reshape(len(places), t_blk, LANES).astype(jnp.bfloat16)
            for k in places:
                out_copy(2 * i, 2 * n, k).start()

        by_pieces(first, count, do)

    ready = set()

    def need(b):
        if b not in ready:
            ready.add(b)
            gathered(b)

    def eager_only(do, at_eager):
        @pl.when(c < eager if at_eager else c >= eager)
        def _():
            do()

    def reach_others():
        @pl.when(c < last)
        def _():
            pl.semaphore_wait(late, last - c)
        z_send(0)

    for o in flat[:-1]:
        y_copy(o).wait_recv()
    own.wait()

    eager_only(reach_others, False)
    early_products(0)
    early_hop(0, 0)
    early_hop(1, 1)
    early_products(1)
    early_hop(1, 0)
    early_hop(0, 1)
    eager_only(reach_others, True)

    def early_event(h):
        if h < 0:
            @pl.when(c < last)
            def _():
                pl.semaphore_wait(go, 1)
            early_finish()
        else:
            for direction in (0, 1):
                early_hop(direction, h)

    for entry in schedule:
        if entry[0] == -2:
            z_send(entry[1])
            if entry[1] == 2:
                @pl.when(c == last)
                def _():
                    pl.semaphore_wait(go, 1)
                    for j in range(last):
                        tell(go, (s, r, j))
            if entry[1] == 1:
                for h in range(2, len(hops)):
                    eager_only(functools.partial(early_event, h), True)
        elif entry[0] == -1:
            if entry[1] < 0:
                early_event(-1)
            else:
                eager_only(functools.partial(early_event, entry[1]), False)
        elif entry[1] < 0:
            finish(entry[0], *entry[2:])
        else:
            is_long, k = hops[entry[1]]
            if entry[0] == 0:
                need(k - 1 if is_long else k)
            slot(*entry)

    def sent(block, sem):
        pltpu.make_async_remote_copy(
            src_ref=block, dst_ref=block, send_sem=sem, recv_sem=tsem,
            device_id=ring_to(0), device_id_type=MESH).wait_send()

    sent(tk.at[0, pl.ds(0, n_row - 1)], ysend)
    sent(tk.at[pl.ds(1, n_col - 1)], zsend)
    sent(sb0, esend)
    for direction in (0, 1):
        for part in (0, 1):
            sent(cut[part][2].at[direction], rsend.at[direction, part])
    sent(hid, osend)
    pltpu.make_async_remote_copy(
        src_ref=out, dst_ref=out, send_sem=osend, recv_sem=orecv,
        device_id=ring_to(0), device_id_type=MESH).wait_recv()


def shards(tokens, gate_weight, up_weight):
    n_sec, n_row, n_col = (lax.axis_size(a) for a in ("section", "row", "col"))
    _, t_blk, features = tokens.shape
    _, depth, width = gate_weight.shape
    units = width // LANES
    half = units // 2
    group = (n_col - 1) * t_blk
    n_hops = n_row - 1
    slots = half * n_hops
    edge = LOW * t_blk
    dma = pltpu.SemaphoreType.DMA
    bf16 = jnp.bfloat16
    return pl.pallas_call(
        functools.partial(kernel, (n_sec, n_row, n_col, SCHEDULE, EAGER, LOW, PIECE)),
        out_shape=jax.ShapeDtypeStruct((1, t_blk, width * n_col), bf16),
        in_specs=[pl.BlockSpec(memory_space=pltpu.HBM)] * 3,
        out_specs=pl.BlockSpec(memory_space=pl.ANY),
        scratch_shapes=[
            pltpu.VMEM((t_blk, features), bf16),
            pltpu.VMEM((depth, 2 * width), bf16),
            pltpu.VMEM((n_col, n_row, t_blk, depth), bf16),
            pltpu.VMEM((n_row, group, depth), bf16),
            pltpu.VMEM((2, half, n_row, t_blk, UNIT), jnp.float32),
            pltpu.VMEM((2, n_hops, half, t_blk, UNIT), bf16),
            pltpu.VMEM((2, n_hops, half, t_blk, UNIT), bf16),
            pltpu.VMEM((n_row, units, group - edge, UNIT), jnp.float32),
            *[pltpu.VMEM((2, slots, edge, UNIT), bf16), pltpu.VMEM((2, slots, group - edge, UNIT), bf16)] * 2,
            pltpu.VMEM((n_col, t_blk, width), bf16),
            dma((units,)), dma, dma, dma((n_row,)), dma, dma((n_row,)), dma, dma((2, n_hops)),
            dma((2, 2)), dma((2, 2, slots)), dma, dma, *[pltpu.SemaphoreType.REGULAR] * 2,
        ],
        compiler_params=pltpu.CompilerParams(
            collective_id=0, has_side_effects=True, vmem_limit_bytes=VMEM_MIB * 1024 * 1024),
    )(tokens, gate_weight, up_weight)


def solution(mesh):
    placed = (P("section", ("row", "col"), None), P("section", "row", "col"), P("section", "row", "col"))
    return jax.shard_map(
        shards, mesh=mesh, in_specs=placed, out_specs=P("section", ("row", "col"), None), check_vma=False)
```

```python
import functools

import jax
import jax.numpy as jnp
from jax import lax
from jax.experimental import pallas as pl
from jax.experimental.pallas import tpu as pltpu
from jax.sharding import PartitionSpec as P

MESH = pl.DeviceIdType.MESH
LANES = 128
UNIT = 2 * LANES
VMEM_MIB = 54
PIECE = 4
LOW = 3
EARLY = ((-2, 1), (0, 0, 0, 7), (-2, 2), (-1, 2), (-1, 3), (1, 0, 0, 7), (-2, 3), (-1, 4), (-1, 5), (0, 1, 0, 7), (0, 2, 0, 7), (-1, 6), (1, 1, 0, 7), (-1, -1))
LATE = ((0, 3, 0, 7), (0, 4, 0, 7), (1, 2, 0, 7), (0, 5, 0, 7), (0, 6, 0, 7), (1, 3, 0, 7), (0, -1, 0, 7), (1, 4, 0, 7), (1, 5, 0, 7), (1, 6, 0, 7), (1, -1, 0, 7))
SCHEDULE = EARLY + LATE
EAGER = 4


def kernel(plan, tokens, gate, up, out, tv, w, tk, tkm, p0, rb0, sb0, kept, rlow, rhigh, slow, shigh, hid,
           wsem, tsem, ysend, yrecv, zsend, zrecv, esend, erecv, rsend, rrecv, osend, orecv, late, go):
    n_sec, n_row, n_col, schedule, eager, low, piece_units = plan
    s, r, c = lax.axis_index("section"), lax.axis_index("row"), lax.axis_index("col")
    t_blk, depth = tk.shape[2], tk.shape[3]
    width = hid.shape[2]
    half = width // LANES // 2
    group = (n_col - 1) * t_blk
    long, short = n_row // 2, n_row // 2 - 1
    nxt, prv = lax.rem(s + 1, n_sec), lax.rem(s + n_sec - 1, n_sec)

    def row_at(offset):
        return lax.rem(r + (offset % n_row), n_row)

    def col_at(offset):
        return lax.rem(c + (offset % n_col), n_col)

    last = n_col - 1

    def tell(sem, device):
        pl.semaphore_signal(sem, inc=1, device_id=device, device_id_type=MESH)

    def unit_cols(u):
        return pl.ds(pl.multiple_of(u * UNIT, UNIT), UNIT)

    stage = pltpu.make_async_copy(tokens.at[0], tv, tsem)
    stage.start()
    barrier = pltpu.get_barrier_semaphore()
    for o in range(1, n_row):
        tell(barrier, (s, row_at(o), c))
    for j in range(1, n_col):
        @pl.when(c < j)
        def _():
            tell(barrier, (s, r, j))

    @pl.when(c == last)
    def _():
        tell(barrier, (nxt, r, last))

    @pl.loop(0, 2 * half)
    def _(u):
        cols = pl.ds(pl.multiple_of(u * LANES, LANES), LANES)
        first = pl.ds(pl.multiple_of(u * UNIT, UNIT), LANES)
        second = pl.ds(pl.multiple_of(u * UNIT + LANES, LANES), LANES)
        pltpu.make_async_copy(gate.at[0, :, cols], w.at[:, first], wsem.at[u]).start()
        pltpu.make_async_copy(up.at[0, :, cols], w.at[:, second], wsem.at[u]).start()

    stage.wait()
    pl.semaphore_wait(barrier, n_row - 1 + c + jnp.where(c == last, 1, 0))

    for j in range(last):
        @pl.when(c > j)
        def _():
            tell(late, (s, r, j))

    @pl.when(c == last)
    def _():
        tell(go, (prv, r, last))

    batches = []
    for d in range(long, 0, -1):
        batches.append([d] if 2 * d == n_row else [d, n_row - d])
    batches[-1].append(0)
    flat = [o for batch in batches for o in batch]
    place = {o: i for i, o in enumerate(flat)}

    def y_copy(o):
        dest = row_at(-o)
        return pltpu.make_async_remote_copy(
            src_ref=tv.at[:, pl.ds(pl.multiple_of(dest * depth, depth), depth)], dst_ref=tk.at[0, place[o]],
            send_sem=ysend, recv_sem=yrecv.at[o], device_id=(s, dest, c), device_id_type=MESH)

    def z_range(b):
        return pl.ds(place[batches[b][0]], len(batches[b]))

    def z_send(b):
        for j in range(n_col):
            @pl.when(c != j)
            def _():
                pltpu.make_async_remote_copy(
                    src_ref=tk.at[0, z_range(b)], dst_ref=tk.at[jnp.where(c < j, c + 1, c), z_range(b)],
                    send_sem=zsend, recv_sem=zrecv.at[b], device_id=(s, r, j), device_id_type=MESH).start()

    def gathered(b):
        block = tk.at[pl.ds(1, n_col - 1), z_range(b)]
        pltpu.make_async_remote_copy(
            src_ref=block, dst_ref=block, send_sem=zsend, recv_sem=zrecv.at[b],
            device_id=(s, r, col_at(1)), device_id_type=MESH).wait_recv()
        for o in batches[b]:
            rows = tk[pl.ds(1, n_col - 1), place[o]].astype(jnp.float32)
            tkm[place[o]] = rows.reshape(group, depth).astype(jnp.bfloat16)

    for o in flat[:-1]:
        y_copy(o).start()
    own = pltpu.make_async_copy(tv.at[:, pl.ds(pl.multiple_of(r * depth, depth), depth)], tk.at[0, place[0]], tsem)
    own.start()

    hops = []
    for k in range(1, long + 1):
        hops.append((True, k))
        if k <= short:
            hops.append((False, k))

    def parity(direction, is_long):
        return 0 if is_long == (direction == 0) else 1

    def source(direction, hop):
        is_long, k = hop
        dist = (long if is_long else short) + 1 - k
        return dist if direction == 0 else n_row - dist

    def ring_to(direction):
        return (s, row_at(1 if direction == 0 else -1), c)

    def out_copy(first, count, k):
        src = pl.ds(pl.multiple_of(first * LANES, LANES), count * LANES)
        dst = pl.ds(pl.multiple_of(c * width + first * LANES, LANES), count * LANES)
        return pltpu.make_async_remote_copy(
            src_ref=hid.at[k, :, src], dst_ref=out.at[0, :, dst], send_sem=osend, recv_sem=orecv,
            device_id=(nxt, r, c if k == 0 else jnp.where(k - 1 < c, k - 1, k)), device_id_type=MESH)

    def gated(value):
        gate_sum, up_sum = value[..., :LANES], value[..., LANES:]
        return gate_sum / (1.0 + jnp.exp(-gate_sum)) * up_sum

    def early_copy(direction, h):
        return pltpu.make_async_remote_copy(
            src_ref=sb0.at[direction, h], dst_ref=rb0.at[direction, h], send_sem=esend, recv_sem=erecv.at[direction, h],
            device_id=ring_to(direction), device_id_type=MESH)

    def early_hop(direction, h):
        is_long, k = hops[h]
        value = p0[parity(direction, is_long), :, place[source(direction, hops[h])]]
        if k > 1:
            before = hops.index((is_long, k - 1))
            early_copy(direction, before).wait_recv()
            value = value + rb0[direction, before].astype(jnp.float32)
        sb0[direction, h] = value.astype(jnp.bfloat16)
        early_copy(direction, h).start()

    def early_products(par):
        rows = tk[0].astype(jnp.float32).reshape(n_row * t_blk, depth).astype(jnp.bfloat16)

        @pl.loop(0, half)
        def _(i):
            u = 2 * i + par
            pltpu.make_async_copy(w.at[:, unit_cols(u)], w.at[:, unit_cols(u)], wsem.at[u]).wait()
            value = jnp.dot(rows, w[:, unit_cols(u)], preferred_element_type=jnp.float32)
            p0[par, i] = value.reshape(n_row, t_blk, UNIT)

    def early_finish():
        for par in (0, 1):
            value = p0[par, :, place[0]]
            for direction in (0, 1):
                is_long = (par == 0) == (direction == 0)
                h = hops.index((is_long, long if is_long else short))
                early_copy(direction, h).wait_recv()
                value = value + rb0[direction, h].astype(jnp.float32)
            result = gated(value)
            for i in range(half):
                u = 2 * i + par
                hid[0, :, u * LANES:(u + 1) * LANES] = result[i].astype(jnp.bfloat16)
        out_copy(0, 2 * half, 0).start()

    edge = low * t_blk
    cut = ((0, edge, slow, rlow), (edge, group - edge, shigh, rhigh))

    def ring_copy(part, direction, index, n):
        _, _, sbuf, rbuf = cut[part]
        return pltpu.make_async_remote_copy(
            src_ref=sbuf.at[direction, pl.ds(index, n)], dst_ref=rbuf.at[direction, pl.ds(index, n)],
            send_sem=rsend.at[direction, part], recv_sem=rrecv.at[direction, part, index],
            device_id=ring_to(direction), device_id_type=MESH)

    def product(part, o, u):
        if part == 1:
            return kept[place[o], u]
        value = jnp.dot(tkm[place[o]], w[:, unit_cols(u)], preferred_element_type=jnp.float32)
        kept[place[o], u] = value[edge:]
        return value[:edge]

    def by_pieces(first, count, do):
        whole = count // piece_units
        if whole:
            @pl.loop(0, whole)
            def _(j):
                do(first + j * piece_units, piece_units)
        if count % piece_units:
            do(first + whole * piece_units, count % piece_units)

    def slot(part, h, first, count):
        is_long, k = hops[h]
        _, _, sbuf, rbuf = cut[part]

        def do(i, n):
            for direction in (0, 1):
                here = h * half + i
                before = hops.index((is_long, k - 1)) * half + i if k > 1 else 0
                o = source(direction, hops[h])
                values = [product(part, o, 2 * (i + e) + parity(direction, is_long)) for e in range(n)]
                if k > 1:
                    ring_copy(part, direction, before, n).wait_recv()
                for e in range(n):
                    value = values[e]
                    if k > 1:
                        value = value + rbuf[direction, before + e].astype(jnp.float32)
                    sbuf[direction, here + e] = value.astype(jnp.bfloat16)
                ring_copy(part, direction, here, n).start()

        by_pieces(first, count, do)

    def finish(part, first, count):
        start, rows, _, rbuf = cut[part]
        places = range(1, 1 + low) if part == 0 else range(1 + low, n_col)

        def do(i, n):
            for par in (0, 1):
                values = [product(part, 0, 2 * (i + e) + par) for e in range(n)]
                for direction in (0, 1):
                    is_long = (par == 0) == (direction == 0)
                    before = hops.index((is_long, long if is_long else short)) * half + i
                    ring_copy(part, direction, before, n).wait_recv()
                    values = [values[e] + rbuf[direction, before + e].astype(jnp.float32) for e in range(n)]
                for e in range(n):
                    u = 2 * (i + e) + par
                    hid[pl.ds(places[0], len(places)), :, pl.ds(pl.multiple_of(u * LANES, LANES), LANES)] = gated(
                        values[e]).reshape(len(places), t_blk, LANES).astype(jnp.bfloat16)
            for k in places:
                out_copy(2 * i, 2 * n, k).start()

        by_pieces(first, count, do)

    ready = set()

    def need(b):
        if b not in ready:
            ready.add(b)
            gathered(b)

    def eager_only(do, at_eager):
        @pl.when(c < eager if at_eager else c >= eager)
        def _():
            do()

    def reach_others():
        @pl.when(c < last)
        def _():
            pl.semaphore_wait(late, last - c)
        z_send(0)

    for o in flat[:-1]:
        y_copy(o).wait_recv()
    own.wait()

    eager_only(reach_others, False)
    early_products(0)
    early_hop(0, 0)
    early_hop(1, 1)
    early_products(1)
    early_hop(1, 0)
    early_hop(0, 1)
    eager_only(reach_others, True)

    def early_event(h):
        if h < 0:
            @pl.when(c < last)
            def _():
                pl.semaphore_wait(go, 1)
            early_finish()
        else:
            for direction in (0, 1):
                early_hop(direction, h)

    for entry in schedule:
        if entry[0] == -2:
            z_send(entry[1])
            if entry[1] == 2:
                @pl.when(c == last)
                def _():
                    pl.semaphore_wait(go, 1)
                    for j in range(last):
                        tell(go, (s, r, j))
            if entry[1] == 1:
                for h in range(2, len(hops)):
                    eager_only(functools.partial(early_event, h), True)
        elif entry[0] == -1:
            if entry[1] < 0:
                early_event(-1)
            else:
                eager_only(functools.partial(early_event, entry[1]), False)
        elif entry[1] < 0:
            finish(entry[0], *entry[2:])
        else:
            is_long, k = hops[entry[1]]
            if entry[0] == 0:
                need(k - 1 if is_long else k)
            slot(*entry)

    def sent(block, sem):
        pltpu.make_async_remote_copy(
            src_ref=block, dst_ref=block, send_sem=sem, recv_sem=tsem,
            device_id=ring_to(0), device_id_type=MESH).wait_send()

    sent(tk.at[0, pl.ds(0, n_row - 1)], ysend)
    sent(tk.at[pl.ds(1, n_col - 1)], zsend)
    sent(sb0, esend)
    for direction in (0, 1):
        for part in (0, 1):
            sent(cut[part][2].at[direction], rsend.at[direction, part])
    sent(hid, osend)
    pltpu.make_async_remote_copy(
        src_ref=out, dst_ref=out, send_sem=osend, recv_sem=orecv,
        device_id=ring_to(0), device_id_type=MESH).wait_recv()


def shards(tokens, gate_weight, up_weight):
    n_sec, n_row, n_col = (lax.axis_size(a) for a in ("section", "row", "col"))
    _, t_blk, features = tokens.shape
    _, depth, width = gate_weight.shape
    units = width // LANES
    half = units // 2
    group = (n_col - 1) * t_blk
    n_hops = n_row - 1
    slots = half * n_hops
    edge = LOW * t_blk
    dma = pltpu.SemaphoreType.DMA
    bf16 = jnp.bfloat16
    return pl.pallas_call(
        functools.partial(kernel, (n_sec, n_row, n_col, SCHEDULE, EAGER, LOW, PIECE)),
        out_shape=jax.ShapeDtypeStruct((1, t_blk, width * n_col), bf16),
        in_specs=[pl.BlockSpec(memory_space=pltpu.HBM)] * 3,
        out_specs=pl.BlockSpec(memory_space=pl.ANY),
        scratch_shapes=[
            pltpu.VMEM((t_blk, features), bf16),
            pltpu.VMEM((depth, 2 * width), bf16),
            pltpu.VMEM((n_col, n_row, t_blk, depth), bf16),
            pltpu.VMEM((n_row, group, depth), bf16),
            pltpu.VMEM((2, half, n_row, t_blk, UNIT), jnp.float32),
            pltpu.VMEM((2, n_hops, half, t_blk, UNIT), bf16),
            pltpu.VMEM((2, n_hops, half, t_blk, UNIT), bf16),
            pltpu.VMEM((n_row, units, group - edge, UNIT), jnp.float32),
            *[pltpu.VMEM((2, slots, edge, UNIT), bf16), pltpu.VMEM((2, slots, group - edge, UNIT), bf16)] * 2,
            pltpu.VMEM((n_col, t_blk, width), bf16),
            dma((units,)), dma, dma, dma((n_row,)), dma, dma((n_row,)), dma, dma((2, n_hops)),
            dma((2, 2)), dma((2, 2, slots)), dma, dma, *[pltpu.SemaphoreType.REGULAR] * 2,
        ],
        compiler_params=pltpu.CompilerParams(
            collective_id=0, has_side_effects=True, vmem_limit_bytes=VMEM_MIB * 1024 * 1024),
    )(tokens, gate_weight, up_weight)


def solution(mesh):
    placed = (P("section", ("row", "col"), None), P("section", "row", "col"), P("section", "row", "col"))
    return jax.shard_map(
        shards, mesh=mesh, in_specs=placed, out_specs=P("section", ("row", "col"), None), check_vma=False)
```

```python
import functools

import jax
import jax.numpy as jnp
from jax import lax
from jax.experimental import pallas as pl
from jax.experimental.pallas import tpu as pltpu
from jax.sharding import PartitionSpec as P

MESH = pl.DeviceIdType.MESH
LANES = 128
UNIT = 2 * LANES
VMEM_MIB = 53
PIECE = 4
LOW = 3
EARLY = ((-2, 1), (0, 0, 0, 7), (-2, 2), (-1, 2), (-1, 3), (1, 0, 0, 7), (-2, 3), (-1, 4), (-1, 5), (0, 1, 0, 7), (0, 2, 0, 7), (-1, 6), (1, 1, 0, 7), (-1, -1))
LATE = ((0, 3, 0, 7), (0, 4, 0, 7), (1, 2, 0, 7), (0, 5, 0, 7), (0, 6, 0, 7), (1, 3, 0, 7), (0, -1, 0, 7), (1, 4, 0, 7), (1, 5, 0, 7), (1, 6, 0, 7), (1, -1, 0, 7))
SCHEDULE = EARLY + LATE
EAGER = 4


def kernel(plan, tokens, gate, up, out, tv, w, tk, tkm, p0, rb0, sb0, kept, rlow, rhigh, slow, shigh, hid,
           wsem, tsem, ysend, yrecv, zsend, zrecv, esend, erecv, rsend, rrecv, osend, orecv, late, go):
    n_sec, n_row, n_col, schedule, eager, low, piece_units = plan
    s, r, c = lax.axis_index("section"), lax.axis_index("row"), lax.axis_index("col")
    t_blk, depth = tk.shape[2], tk.shape[3]
    width = hid.shape[2]
    half = width // LANES // 2
    group = (n_col - 1) * t_blk
    long, short = n_row // 2, n_row // 2 - 1
    nxt, prv = lax.rem(s + 1, n_sec), lax.rem(s + n_sec - 1, n_sec)

    def row_at(offset):
        return lax.rem(r + (offset % n_row), n_row)

    def col_at(offset):
        return lax.rem(c + (offset % n_col), n_col)

    last = n_col - 1

    def tell(sem, device):
        pl.semaphore_signal(sem, inc=1, device_id=device, device_id_type=MESH)

    def unit_cols(u):
        return pl.ds(pl.multiple_of(u * UNIT, UNIT), UNIT)

    stage = pltpu.make_async_copy(tokens.at[0], tv, tsem)
    stage.start()
    barrier = pltpu.get_barrier_semaphore()
    for o in range(1, n_row):
        tell(barrier, (s, row_at(o), c))
    for j in range(1, n_col):
        @pl.when(c < j)
        def _():
            tell(barrier, (s, r, j))

    @pl.when(c == last)
    def _():
        tell(barrier, (nxt, r, last))

    @pl.loop(0, 2 * half)
    def _(u):
        cols = pl.ds(pl.multiple_of(u * LANES, LANES), LANES)
        first = pl.ds(pl.multiple_of(u * UNIT, UNIT), LANES)
        second = pl.ds(pl.multiple_of(u * UNIT + LANES, LANES), LANES)
        pltpu.make_async_copy(gate.at[0, :, cols], w.at[:, first], wsem.at[u]).start()
        pltpu.make_async_copy(up.at[0, :, cols], w.at[:, second], wsem.at[u]).start()

    stage.wait()
    pl.semaphore_wait(barrier, n_row - 1 + c + jnp.where(c == last, 1, 0))

    for j in range(last):
        @pl.when(c > j)
        def _():
            tell(late, (s, r, j))

    @pl.when(c == last)
    def _():
        tell(go, (prv, r, last))

    batches = []
    for d in range(long, 0, -1):
        batches.append([d] if 2 * d == n_row else [d, n_row - d])
    batches[-1].append(0)
    flat = [o for batch in batches for o in batch]
    place = {o: i for i, o in enumerate(flat)}

    def y_copy(o):
        dest = row_at(-o)
        return pltpu.make_async_remote_copy(
            src_ref=tv.at[:, pl.ds(pl.multiple_of(dest * depth, depth), depth)], dst_ref=tk.at[0, place[o]],
            send_sem=ysend, recv_sem=yrecv.at[o], device_id=(s, dest, c), device_id_type=MESH)

    def z_range(b):
        return pl.ds(place[batches[b][0]], len(batches[b]))

    def z_send(b):
        for j in range(n_col):
            @pl.when(c != j)
            def _():
                pltpu.make_async_remote_copy(
                    src_ref=tk.at[0, z_range(b)], dst_ref=tk.at[jnp.where(c < j, c + 1, c), z_range(b)],
                    send_sem=zsend, recv_sem=zrecv.at[b], device_id=(s, r, j), device_id_type=MESH).start()

    def gathered(b):
        block = tk.at[pl.ds(1, n_col - 1), z_range(b)]
        pltpu.make_async_remote_copy(
            src_ref=block, dst_ref=block, send_sem=zsend, recv_sem=zrecv.at[b],
            device_id=(s, r, col_at(1)), device_id_type=MESH).wait_recv()
        for o in batches[b]:
            rows = tk[pl.ds(1, n_col - 1), place[o]].astype(jnp.float32)
            tkm[place[o]] = rows.reshape(group, depth).astype(jnp.bfloat16)

    for o in flat[:-1]:
        y_copy(o).start()
    own = pltpu.make_async_copy(tv.at[:, pl.ds(pl.multiple_of(r * depth, depth), depth)], tk.at[0, place[0]], tsem)
    own.start()

    hops = []
    for k in range(1, long + 1):
        hops.append((True, k))
        if k <= short:
            hops.append((False, k))

    def parity(direction, is_long):
        return 0 if is_long == (direction == 0) else 1

    def source(direction, hop):
        is_long, k = hop
        dist = (long if is_long else short) + 1 - k
        return dist if direction == 0 else n_row - dist

    def ring_to(direction):
        return (s, row_at(1 if direction == 0 else -1), c)

    def out_copy(first, count, k):
        src = pl.ds(pl.multiple_of(first * LANES, LANES), count * LANES)
        dst = pl.ds(pl.multiple_of(c * width + first * LANES, LANES), count * LANES)
        return pltpu.make_async_remote_copy(
            src_ref=hid.at[k, :, src], dst_ref=out.at[0, :, dst], send_sem=osend, recv_sem=orecv,
            device_id=(nxt, r, c if k == 0 else jnp.where(k - 1 < c, k - 1, k)), device_id_type=MESH)

    def gated(value):
        gate_sum, up_sum = value[..., :LANES], value[..., LANES:]
        return gate_sum / (1.0 + jnp.exp(-gate_sum)) * up_sum

    def early_copy(direction, h):
        return pltpu.make_async_remote_copy(
            src_ref=sb0.at[direction, h], dst_ref=rb0.at[direction, h], send_sem=esend, recv_sem=erecv.at[direction, h],
            device_id=ring_to(direction), device_id_type=MESH)

    def early_hop(direction, h):
        is_long, k = hops[h]
        value = p0[parity(direction, is_long), :, place[source(direction, hops[h])]]
        if k > 1:
            before = hops.index((is_long, k - 1))
            early_copy(direction, before).wait_recv()
            value = value + rb0[direction, before].astype(jnp.float32)
        sb0[direction, h] = value.astype(jnp.bfloat16)
        early_copy(direction, h).start()

    def early_products(par):
        rows = tk[0].astype(jnp.float32).reshape(n_row * t_blk, depth).astype(jnp.bfloat16)

        @pl.loop(0, half)
        def _(i):
            u = 2 * i + par
            pltpu.make_async_copy(w.at[:, unit_cols(u)], w.at[:, unit_cols(u)], wsem.at[u]).wait()
            value = jnp.dot(rows, w[:, unit_cols(u)], preferred_element_type=jnp.float32)
            p0[par, i] = value.reshape(n_row, t_blk, UNIT)

    def early_finish():
        for par in (0, 1):
            value = p0[par, :, place[0]]
            for direction in (0, 1):
                is_long = (par == 0) == (direction == 0)
                h = hops.index((is_long, long if is_long else short))
                early_copy(direction, h).wait_recv()
                value = value + rb0[direction, h].astype(jnp.float32)
            result = gated(value)
            for i in range(half):
                u = 2 * i + par
                hid[0, :, u * LANES:(u + 1) * LANES] = result[i].astype(jnp.bfloat16)
        out_copy(0, 2 * half, 0).start()

    edge = low * t_blk
    cut = ((0, edge, slow, rlow), (edge, group - edge, shigh, rhigh))

    def ring_copy(part, direction, index, n):
        _, _, sbuf, rbuf = cut[part]
        return pltpu.make_async_remote_copy(
            src_ref=sbuf.at[direction, pl.ds(index, n)], dst_ref=rbuf.at[direction, pl.ds(index, n)],
            send_sem=rsend.at[direction, part], recv_sem=rrecv.at[direction, part, index],
            device_id=ring_to(direction), device_id_type=MESH)

    def product(part, o, u):
        if part == 1:
            return kept[place[o], u]
        value = jnp.dot(tkm[place[o]], w[:, unit_cols(u)], preferred_element_type=jnp.float32)
        kept[place[o], u] = value[edge:]
        return value[:edge]

    def by_pieces(first, count, do):
        whole = count // piece_units
        if whole:
            @pl.loop(0, whole)
            def _(j):
                do(first + j * piece_units, piece_units)
        if count % piece_units:
            do(first + whole * piece_units, count % piece_units)

    def slot(part, h, first, count):
        is_long, k = hops[h]
        _, _, sbuf, rbuf = cut[part]

        def do(i, n):
            for direction in (0, 1):
                here = h * half + i
                before = hops.index((is_long, k - 1)) * half + i if k > 1 else 0
                o = source(direction, hops[h])
                values = [product(part, o, 2 * (i + e) + parity(direction, is_long)) for e in range(n)]
                if k > 1:
                    ring_copy(part, direction, before, n).wait_recv()
                for e in range(n):
                    value = values[e]
                    if k > 1:
                        value = value + rbuf[direction, before + e].astype(jnp.float32)
                    sbuf[direction, here + e] = value.astype(jnp.bfloat16)
                ring_copy(part, direction, here, n).start()

        by_pieces(first, count, do)

    def finish(part, first, count):
        start, rows, _, rbuf = cut[part]
        places = range(1, 1 + low) if part == 0 else range(1 + low, n_col)

        def do(i, n):
            for par in (0, 1):
                values = [product(part, 0, 2 * (i + e) + par) for e in range(n)]
                for direction in (0, 1):
                    is_long = (par == 0) == (direction == 0)
                    before = hops.index((is_long, long if is_long else short)) * half + i
                    ring_copy(part, direction, before, n).wait_recv()
                    values = [values[e] + rbuf[direction, before + e].astype(jnp.float32) for e in range(n)]
                for e in range(n):
                    u = 2 * (i + e) + par
                    hid[pl.ds(places[0], len(places)), :, pl.ds(pl.multiple_of(u * LANES, LANES), LANES)] = gated(
                        values[e]).reshape(len(places), t_blk, LANES).astype(jnp.bfloat16)
            for k in places:
                out_copy(2 * i, 2 * n, k).start()

        by_pieces(first, count, do)

    ready = set()

    def need(b):
        if b not in ready:
            ready.add(b)
            gathered(b)

    def eager_only(do, at_eager):
        @pl.when(c < eager if at_eager else c >= eager)
        def _():
            do()

    def reach_others():
        @pl.when(c < last)
        def _():
            pl.semaphore_wait(late, last - c)
        z_send(0)

    for o in flat[:-1]:
        y_copy(o).wait_recv()
    own.wait()

    eager_only(reach_others, False)
    early_products(0)
    early_hop(0, 0)
    early_hop(1, 1)
    early_products(1)
    early_hop(1, 0)
    early_hop(0, 1)
    eager_only(reach_others, True)

    def early_event(h):
        if h < 0:
            @pl.when(c < last)
            def _():
                pl.semaphore_wait(go, 1)
            early_finish()
        else:
            for direction in (0, 1):
                early_hop(direction, h)

    for entry in schedule:
        if entry[0] == -2:
            z_send(entry[1])
            if entry[1] == 2:
                @pl.when(c == last)
                def _():
                    pl.semaphore_wait(go, 1)
                    for j in range(last):
                        tell(go, (s, r, j))
            if entry[1] == 1:
                for h in range(2, len(hops)):
                    eager_only(functools.partial(early_event, h), True)
        elif entry[0] == -1:
            if entry[1] < 0:
                early_event(-1)
            else:
                eager_only(functools.partial(early_event, entry[1]), False)
        elif entry[1] < 0:
            finish(entry[0], *entry[2:])
        else:
            is_long, k = hops[entry[1]]
            if entry[0] == 0:
                need(k - 1 if is_long else k)
            slot(*entry)

    def sent(block, sem):
        pltpu.make_async_remote_copy(
            src_ref=block, dst_ref=block, send_sem=sem, recv_sem=tsem,
            device_id=ring_to(0), device_id_type=MESH).wait_send()

    sent(tk.at[0, pl.ds(0, n_row - 1)], ysend)
    sent(tk.at[pl.ds(1, n_col - 1)], zsend)
    sent(sb0, esend)
    for direction in (0, 1):
        for part in (0, 1):
            sent(cut[part][2].at[direction], rsend.at[direction, part])
    sent(hid, osend)
    pltpu.make_async_remote_copy(
        src_ref=out, dst_ref=out, send_sem=osend, recv_sem=orecv,
        device_id=ring_to(0), device_id_type=MESH).wait_recv()


def shards(tokens, gate_weight, up_weight):
    n_sec, n_row, n_col = (lax.axis_size(a) for a in ("section", "row", "col"))
    _, t_blk, features = tokens.shape
    _, depth, width = gate_weight.shape
    units = width // LANES
    half = units // 2
    group = (n_col - 1) * t_blk
    n_hops = n_row - 1
    slots = half * n_hops
    edge = LOW * t_blk
    dma = pltpu.SemaphoreType.DMA
    bf16 = jnp.bfloat16
    return pl.pallas_call(
        functools.partial(kernel, (n_sec, n_row, n_col, SCHEDULE, EAGER, LOW, PIECE)),
        out_shape=jax.ShapeDtypeStruct((1, t_blk, width * n_col), bf16),
        in_specs=[pl.BlockSpec(memory_space=pltpu.HBM)] * 3,
        out_specs=pl.BlockSpec(memory_space=pl.ANY),
        scratch_shapes=[
            pltpu.VMEM((t_blk, features), bf16),
            pltpu.VMEM((depth, 2 * width), bf16),
            pltpu.VMEM((n_col, n_row, t_blk, depth), bf16),
            pltpu.VMEM((n_row, group, depth), bf16),
            pltpu.VMEM((2, half, n_row, t_blk, UNIT), jnp.float32),
            pltpu.VMEM((2, n_hops, half, t_blk, UNIT), bf16),
            pltpu.VMEM((2, n_hops, half, t_blk, UNIT), bf16),
            pltpu.VMEM((n_row, units, group - edge, UNIT), jnp.float32),
            *[pltpu.VMEM((2, slots, edge, UNIT), bf16), pltpu.VMEM((2, slots, group - edge, UNIT), bf16)] * 2,
            pltpu.VMEM((n_col, t_blk, width), bf16),
            dma((units,)), dma, dma, dma((n_row,)), dma, dma((n_row,)), dma, dma((2, n_hops)),
            dma((2, 2)), dma((2, 2, slots)), dma, dma, *[pltpu.SemaphoreType.REGULAR] * 2,
        ],
        compiler_params=pltpu.CompilerParams(
            collective_id=0, has_side_effects=True, vmem_limit_bytes=VMEM_MIB * 1024 * 1024),
    )(tokens, gate_weight, up_weight)


def solution(mesh):
    placed = (P("section", ("row", "col"), None), P("section", "row", "col"), P("section", "row", "col"))
    return jax.shard_map(
        shards, mesh=mesh, in_specs=placed, out_specs=P("section", ("row", "col"), None), check_vma=False)
```
